32 devices in a mesh: tm: 8 (over z, x), rows: 4 (over y, core).
Axes of the slice: x: 2, y: 2, z: 4, core: 2. Of those that a mesh axis runs over, the one named last changes fastest.
Arguments:
- video: bfloat16 [64, 32, 128, 128], P('tm', 'rows'), may hold values from -36 to 50
- conv_weight: bfloat16 [3, 3, 3, 128, 256], replicated, may hold values from -0.109375 to 0.109375
- norm_gain: float32 [256], replicated, may hold values from 0.5 to 1.5
- norm_bias: float32 [256], replicated, may hold values from -3 to 3
Outputs:
- patch_tokens: bfloat16 [16, 64, 64, 1024], P('rows', 'tm')
The draws below stay inside these ranges and needn't reach their ends.
All inputs are finite; a program needn't handle non-finite values.
Results may differ from the reference program's by a relative error of at most 0.0049.
Values may be sent and summed in bfloat16 or wider, within the bound.
No kernel may reach another device: no remote copies, remote signals or barrier semaphores. Data moves between devices by JAX's collectives and lax.ppermute only.
A program may use at most 128 MiB of HBM per device.

```python
import jax
import jax.numpy as jnp
from jax import lax

C_IN = 128
CO = 256
GROUPS = 32
F_DEV = 8
W = 128
FRAMES = 64
NH = 32
N_TM = 8


def draw_video(key, part):
    key_noise = jax.random.fold_in(key, 11)
    key_channel = jax.random.fold_in(key, 12)
    full_shape = (FRAMES, NH, W, C_IN)
    frame_pos = jnp.arange(FRAMES, dtype=jnp.float32) / max(FRAMES - 1, 1)
    channel_scale = jnp.exp(jax.random.uniform(key_channel, (C_IN,), jnp.float32, jnp.log(0.5), jnp.log(2.0)))
    ramp = jnp.exp(frame_pos * jnp.log(3.0))
    noise = jnp.clip(jax.random.normal(key_noise, full_shape, jnp.float32), -6.0, 6.0) + 1.0
    return (noise * ramp[:, None, None, None] * channel_scale).astype(jnp.bfloat16)


def normal_values(rng, dims, scale, bound, kind=jnp.bfloat16):
    array = jax.random.normal(rng, dims, jnp.float32) * scale
    return jnp.minimum(jnp.maximum(array, -bound), bound).astype(kind)


def setup_inputs(seed: int = 0) -> dict:
    streams_of = jax.random.split(jax.random.key(seed), 5)
    return {
        "video": draw_video(jax.random.fold_in(streams_of[4], 71), 0),
        "conv_weight": normal_values(streams_of[1], (3, 3, 3, C_IN, CO), (27 * C_IN) ** -0.5, 0.109375),
        "norm_gain": jnp.clip(1.0 + 0.1 * jax.random.normal(streams_of[2], (CO,), jnp.float32), 0.5, 1.5),
        "norm_bias": normal_values(streams_of[3], (CO,), 0.5, 3.0, jnp.float32),
    }


inv_root = 0.7071067811865476

def reference(video, conv_weight, norm_gain, norm_bias):
    blocks = N_TM
    current = video.astype(jnp.float32).reshape(blocks, F_DEV, -1)
    for level_bit in range(3):
        span = 2 ** level_bit
        arranged = current.reshape(blocks // (2 * span), 2, span, F_DEV, -1)
        first_half = arranged[:, 0]
        second_half = arranged[:, 1]
        current = jnp.stack(((first_half + second_half) * inv_root, (first_half - second_half) * inv_root), 1)
        current = current.reshape(blocks, F_DEV, -1)
    wavelet = current.reshape(FRAMES, NH, W, C_IN).astype(jnp.bfloat16)
    padded = jnp.pad(wavelet.astype(jnp.float32), ((2, 0), (1, 1), (1, 1), (0, 0)))
    convolved = lax.conv_general_dilated(padded[None], conv_weight.astype(jnp.float32), (1, 1, 1), 'VALID', dimension_numbers=('NDHWC', 'DHWIO', 'NDHWC'), precision=lax.Precision.HIGHEST)[0]
    groups = convolved.reshape(FRAMES, NH, W, GROUPS, CO // GROUPS)
    group_mean = lax.optimization_barrier(jnp.mean(groups, axis=(0, 1, 2, 4), keepdims=True))
    centered = groups - group_mean
    variance = lax.optimization_barrier(jnp.mean(centered * centered, axis=(0, 1, 2, 4), keepdims=True))
    normed = (centered / jnp.sqrt(variance + 1e-05)).reshape(FRAMES, NH, W, CO)
    activated = jax.nn.silu(normed * norm_gain + norm_bias).astype(jnp.bfloat16)
    arranged = activated.reshape(FRAMES, NH // 2, 2, W // 2, 2, CO).transpose(1, 3, 0, 2, 4, 5)
    return arranged.reshape(NH // 2, W // 2, FRAMES, 4 * CO)
```

```python
import functools

import jax
import jax.numpy as jnp
from jax import lax
from jax.experimental import pallas as pl
from jax.experimental.pallas import tpu as pltpu
from jax.sharding import PartitionSpec as P

GROUPS = 32
LEVELS = 3
TAPS = 3
inv_root = 0.7071067811865476
F32 = jnp.float32
BF16 = jnp.bfloat16
VMEM = pl.BlockSpec(memory_space=pltpu.VMEM)
SMEM = pl.BlockSpec(memory_space=pltpu.SMEM)
MIB = 1 << 20


def shape(dims, dtype):
    return jax.ShapeDtypeStruct(dims, dtype)


def on_core(body, outs, scalar, arrays, scratch=(), flops=0, limit=48):
    moved = sum(a.size * a.dtype.itemsize for a in arrays)
    moved += sum(o.size * jnp.dtype(o.dtype).itemsize for o in outs)
    return pl.pallas_call(
        body,
        out_shape=outs,
        in_specs=[SMEM] + [VMEM] * len(arrays),
        out_specs=[VMEM] * len(outs),
        scratch_shapes=list(scratch),
        compiler_params=pltpu.CompilerParams(vmem_limit_bytes=limit * MIB),
        cost_estimate=pl.CostEstimate(flops=flops, bytes_accessed=moved, transcendentals=0),
    )(scalar, *arrays)


def swap_bit(block, axis, bit):
    count = lax.axis_size(axis)
    return lax.ppermute(block, axis, [(i, i ^ (1 << bit)) for i in range(count)])


def bit_of(me, bit):
    return (me >> bit) & 1


class High:
    def __init__(self, count, width):
        self.bits = count.bit_length() - 1
        self.width = width
        self.order = list(range(self.bits))[::-1]
        self.columns = width // count

    def start(self, me, holder, bit, mine):
        top = self.bits if holder is None else holder
        low = max(bit, 0)
        at = sum(bit_of(me, m) * (self.width >> (self.bits - m)) for m in range(low + (0 if mine else 1), top))
        if not mine:
            at = at + (1 - bit_of(me, bit)) * (self.width >> (self.bits - bit))
        return at

    def length(self, bit):
        return (self.width >> (self.bits - bit)) + 2

    def view(self, ref, holder, source, at, size):
        return ref[pl.ds(at, size)] if holder is None else ref[source, pl.ds(at, size)]

    def sent_shape(self, bit):
        return (1 << (self.bits - 1 - bit), self.length(bit))

    def put(self, out, source, value):
        out[source] = value


class Low:
    def __init__(self, count, width):
        self.count = count
        self.bits = count.bit_length() - 1
        self.width = width
        self.order = list(range(self.bits))
        self.columns = width // count

    def start(self, me, holder, bit, mine):
        bottom = 0 if holder is None else holder + 1
        top = self.bits if mine else bit
        at = sum(bit_of(me, m) * (self.count >> (m + 1)) for m in range(bottom, top))
        if not mine:
            at = at + (1 - bit_of(me, bit)) * (self.count >> (bit + 1))
        return at

    def view(self, ref, holder, source, at, size):
        return ref[pl.ds(at, size)] if holder is None else ref[source, pl.ds(at, size)]

    def length(self, bit):
        return self.count >> (bit + 1)

    def sent_shape(self, bit):
        return (1 << bit, self.length(bit), self.columns + 2)

    def put(self, out, source, value):
        out[source] = value


def sources_of(plan, upto):
    held = [(None, 0, 0)]
    for bit in plan.order[:upto]:
        held += [(bit, i, mask ^ (1 << bit)) for i, (_, _, mask) in enumerate(list(held))]
    return held


def split_body(plan, me_ref, first, second, own, sent, *spare):
    me = me_ref[0]
    width = first.shape[2]
    rows = jnp.swapaxes(jnp.concatenate([first[:, 0], second[:, 0]], 0), 0, 1)
    edge = jnp.zeros((1,) + rows.shape[1:], BF16)
    wide = spare[0] if spare else own
    wide[0:1] = edge
    wide[1 : width + 1] = rows
    wide[width + 1 : width + 2] = edge
    bit = plan.order[0]
    if spare:
        for d in range(plan.count):
            place = sum(((d >> m) & 1) * (plan.count >> (m + 1)) for m in range(plan.bits))
            own[place] = wide[d * plan.columns : (d + 1) * plan.columns + 2]
    sent[0] = own[pl.ds(plan.start(me, None, bit, False), plan.length(bit))]


def split_rows(plan, me, video, pair):
    frames, _, width, channels = video.shape
    low = isinstance(plan, Low)
    bit = plan.order[0]
    own = (plan.count, plan.columns + 2) if low else (width + 2,)
    tail = (2 * frames, channels)
    return pl.pallas_call(
        functools.partial(split_body, plan),
        grid=(1,),
        out_shape=[shape(own + tail, BF16), shape(plan.sent_shape(bit) + tail, BF16)],
        in_specs=[
            SMEM,
            pl.BlockSpec((frames, 1, width, channels), lambda g, h=pair[0]: (0, h, 0, 0)),
            pl.BlockSpec((frames, 1, width, channels), lambda g, h=pair[1]: (0, h, 0, 0)),
        ],
        out_specs=[VMEM, VMEM],
        scratch_shapes=[pltpu.VMEM((width + 2,) + tail, BF16)] if low else [],
        compiler_params=pltpu.CompilerParams(vmem_limit_bytes=24 * MIB),
    )(me, video, video)


def part_body(plan, step, me_ref, *refs):
    me = me_ref[0]
    out = refs[-1]
    holders = dict(zip([None] + plan.order[:step], refs))
    bit = plan.order[step]
    for place, (holder, source, _) in enumerate(sources_of(plan, step)):
        at = plan.start(me, holder, bit, False)
        plan.put(out, place, plan.view(holders[holder], holder, source, at, plan.length(bit)))


def transpose_blocks(plan, me, own, sent):
    got = []
    tail = own.shape[-2:]
    for step, bit in enumerate(plan.order):
        if step:
            outs = [shape(plan.sent_shape(bit) + tail, BF16)]
            (sent,) = on_core(functools.partial(part_body, plan, step), outs, me, [own] + got, limit=24)
        got.append(swap_bit(sent, "tm", bit))
    return [own] + got


def gather(plan, me, refs, blocks):
    holders = dict(zip([None] + plan.order, refs))
    size = plan.columns + 2
    for holder, source, mask in sources_of(plan, plan.bits):
        ref = holders[holder]
        at = plan.start(me, holder, -1, True)
        if isinstance(plan, High):
            value = plan.view(ref, holder, source, at, size)
        else:
            value = ref[at] if holder is None else ref[source, at]
        blocks[me ^ mask] = value


def widen(wide, row, column, cells):
    channels = cells.shape[1]
    frame = lax.broadcasted_iota(jnp.int32, cells.shape, 0)
    for tap in range(TAPS):
        back = TAPS - 1 - tap
        moved = cells
        if back:
            moved = jnp.where(frame < back, 0.0, pltpu.roll(cells, back, 0))
        wide[row, column, :, tap * channels : (tap + 1) * channels] = moved.astype(BF16)


def wavelet_rows(blocks, wide, plain=None):
    count, columns, both, _ = blocks.shape
    frames = both // 2

    def column(i, _):
        values = [blocks[b, i].astype(F32) for b in range(count)]
        for level in range(LEVELS):
            span = 1 << level
            later = list(values)
            for b in range(count):
                if not b & span:
                    later[b] = (values[b] + values[b + span]) * inv_root
                    later[b + span] = (values[b] - values[b + span]) * inv_root
            values = later
        for row in range(2):
            cells = jnp.concatenate([v[row * frames : (row + 1) * frames] for v in values], 0)
            widen(wide, row, i, cells)
            if plain is not None:
                plain[row, i] = cells.astype(BF16)
        return 0

    lax.fori_loop(0, columns, column, 0)


def outer_body(plan, me_ref, *refs):
    *held, wide, plain, blocks = refs
    gather(plan, me_ref[0], held, blocks)
    wavelet_rows(blocks, wide, plain)


def taps(w_ref, terms, before=None):
    columns = terms[0][0].shape[1] - 2
    left, right = [], []
    for wide, row, i in terms:
        for j in range(TAPS):
            cells = wide[row, pl.ds(j, columns)]
            left.append(cells.reshape(-1, cells.shape[-1]))
            right += [w_ref[k, i, j] for k in range(TAPS)]
    total = jnp.dot(
        jnp.concatenate(left, -1), jnp.concatenate(right, 0), preferred_element_type=F32
    )
    if before is not None:
        total = total + before
    return total


def row_sums(total):
    mean = jnp.sum(total, 0, keepdims=True) * (1.0 / total.shape[0])
    apart = total - mean
    return mean, jnp.sum(apart * apart, 0, keepdims=True)


def finish(total, out, sums, row):
    out[row] = total.reshape(out.shape[1:])
    mean, squares = row_sums(total)
    sums[row, 0:1] = mean
    sums[row, 1:2] = squares


def keep(total, out, row):
    out[row] = total.reshape(out.shape[1:])


def flat(ref, row):
    return ref[row].reshape(-1, ref.shape[-1])


def stage_a(plan, me_ref, w_ref, outer, above, below, *refs):
    *held, done, part1, part2, sums, wide, halo, blocks = refs
    gather(plan, me_ref[0], held, blocks)
    wavelet_rows(blocks, wide)

    def column(i, _):
        widen(halo, 0, i, above[i].astype(F32))
        widen(halo, 1, i, below[i].astype(F32))
        return 0

    lax.fori_loop(0, above.shape[0], column, 0)
    finish(taps(w_ref, [(halo, 0, 0), (outer, 0, 1), (wide, 0, 2)]), done, sums, 0)
    finish(taps(w_ref, [(wide, 1, 0), (outer, 1, 1), (halo, 1, 2)]), done, sums, 1)
    keep(taps(w_ref, [(outer, 0, 0), (wide, 0, 1)]), part1, 0)
    keep(taps(w_ref, [(wide, 1, 1), (outer, 1, 2)]), part1, 1)
    keep(taps(w_ref, [(wide, 0, 0)]), part2, 0)
    keep(taps(w_ref, [(wide, 1, 2)]), part2, 1)


def stage_b(plan, me_ref, w_ref, part1, part2, *refs):
    *held, done, next2, part3, sums, wide, blocks = refs
    gather(plan, me_ref[0], held, blocks)
    wavelet_rows(blocks, wide)
    finish(taps(w_ref, [(wide, 0, 2)], flat(part1, 0)), done, sums, 0)
    finish(taps(w_ref, [(wide, 1, 0)], flat(part1, 1)), done, sums, 1)
    keep(taps(w_ref, [(wide, 0, 1)], flat(part2, 0)), next2, 0)
    keep(taps(w_ref, [(wide, 1, 1)], flat(part2, 1)), next2, 1)
    keep(taps(w_ref, [(wide, 0, 0)]), part3, 0)
    keep(taps(w_ref, [(wide, 1, 2)]), part3, 1)


def stage_c(plan, me_ref, w_ref, part2, part3, sums_a, sums_b, *refs):
    *held, done2, done3, message, sums, wide, blocks = refs
    gather(plan, me_ref[0], held, blocks)
    wavelet_rows(blocks, wide)
    finish(taps(w_ref, [(wide, 0, 2)], flat(part2, 0)), done2, sums, 0)
    finish(taps(w_ref, [(wide, 1, 0)], flat(part2, 1)), done2, sums, 1)
    finish(taps(w_ref, [(wide, 0, 1), (wide, 1, 2)], flat(part3, 0)), done3, sums.at[2:4], 0)
    finish(taps(w_ref, [(wide, 0, 0), (wide, 1, 1)], flat(part3, 1)), done3, sums.at[2:4], 1)
    rows = [sums[r] for r in range(4)]
    rows += [s[r] for s in (sums_a, sums_b) for r in range(2)]
    entries = wide.shape[2] * (wide.shape[1] - 2)
    mean = sum(r[0:1] for r in rows) * (1.0 / len(rows))
    squares = sum(r[1:2] + entries * (r[0:1] - mean) * (r[0:1] - mean) for r in rows)
    lanes = message.shape[-1]
    parts = [v[:, c : c + lanes] for v in (mean, squares) for c in range(0, mean.shape[1], lanes)]
    packed = jnp.concatenate(parts + [jnp.zeros((8 - len(parts), lanes), F32)], 0)
    message[...] = jnp.broadcast_to(packed[None], message.shape)


def over_group(values, size):
    lanes = values.shape[-1]
    lane = lax.broadcasted_iota(jnp.int32, values.shape, values.ndim - 1)
    step = 1
    while step < size:
        axis = values.ndim - 1
        down = pltpu.roll(values, step, axis)
        up = pltpu.roll(values, lanes - step, axis)
        values = values + jnp.where((lane & step) != 0, down, up)
        step *= 2
    return values


def norm_body(entries, size, all_ref, gain_ref, bias_ref, *refs):
    *rows, out, affine = refs

    @pl.when(pl.program_id(0) == 0)
    def _():
        devices = all_ref.shape[0]
        half = gain_ref.shape[0]
        means = all_ref[:, 0:half]
        mean = jnp.sum(means, 0) * (1.0 / devices)
        apart = means - mean[None]
        squares = jnp.sum(all_ref[:, half : 2 * half] + entries * apart * apart, 0)
        group_mean = over_group(mean, size) * (1.0 / size)
        apart = mean - group_mean
        group = over_group(squares + (entries * devices) * apart * apart, size)
        variance = group * (1.0 / (entries * devices * size))
        scale = (0.5 * gain_ref[...]) / jnp.sqrt(variance + 1e-05)
        for p in range(half):
            lanes = slice(p * scale.shape[1], (p + 1) * scale.shape[1])
            affine[0:1, lanes] = group_mean[p : p + 1]
            affine[1:2, lanes] = scale[p : p + 1]
            affine[2:3, lanes] = 0.5 * bias_ref[p : p + 1]

    mean, scale, bias = affine[0:1], affine[1:2], affine[2:3]
    channels = mean.shape[1]
    height = 2 * len(rows)
    for h in range(height):
        ref, place = (rows[h], 0) if h < len(rows) else (rows[height - 1 - h], 1)
        for w in range(ref.shape[1]):
            half_v = (ref[place, w] - mean) * scale + bias
            value = half_v + half_v * jnp.tanh(half_v)
            lanes = (h % 2 * 2 + w % 2) * channels
            out[h // 2, w // 2, :, lanes : lanes + channels] = value.astype(BF16)


def per_device(video, conv_weight, norm_gain, norm_bias):
    frames, height, width, channels = video.shape
    outputs = conv_weight.shape[-1]
    count = lax.axis_size("tm")
    strips = lax.axis_size("rows")
    devices = count * strips
    columns = width // count
    time = frames * count
    me = lax.axis_index("tm").astype(jnp.int32).reshape(1)
    high, low = High(count, width), Low(count, width)

    def gathered(plan, pair):
        return transpose_blocks(plan, me, *split_rows(plan, me, video, pair))

    held0 = gathered(high, (0, 7))
    held1 = gathered(high, (1, 6))
    held2 = gathered(low, (2, 5))
    held3 = gathered(low, (3, 4))

    blocks = pltpu.VMEM((count, columns + 2, 2 * frames, channels), BF16)
    wide = (2, columns + 2, time, TAPS * channels)
    wide_spare = pltpu.VMEM(wide, BF16)
    row_pair = shape((2, columns, time, outputs), F32)
    pair_sums = shape((2, 2, outputs), F32)
    tap_flops = 2 * columns * time * TAPS * TAPS * channels * outputs

    outer, plain = on_core(
        functools.partial(outer_body, high),
        [shape(wide, BF16), shape((2, columns + 2, time, channels), BF16)],
        me,
        held0,
        [blocks],
    )
    down = [(i, i + 1) for i in range(strips - 1)]
    up = [(i + 1, i) for i in range(strips - 1)]
    above = lax.ppermute(plain[1], "rows", down)
    below = lax.ppermute(plain[0], "rows", up)
    done0, part1, part2, sums_a = on_core(
        functools.partial(stage_a, high),
        [row_pair, row_pair, row_pair, pair_sums],
        me,
        [conv_weight, outer, above, below] + held1,
        [wide_spare, wide_spare, blocks],
        flops=12 * tap_flops,
    )
    done1, part2, part3, sums_b = on_core(
        functools.partial(stage_b, low),
        [row_pair, row_pair, row_pair, pair_sums],
        me,
        [conv_weight, part1, part2] + held2,
        [wide_spare, blocks],
        flops=6 * tap_flops,
    )
    done2, done3, message = on_core(
        functools.partial(stage_c, low),
        [row_pair, row_pair, shape((devices, 8, 128), F32)],
        me,
        [conv_weight, part2, part3, sums_a, sums_b] + held3,
        [pltpu.VMEM((4, 2, outputs), F32), wide_spare, blocks],
        flops=6 * tap_flops,
    )
    messages = lax.all_to_all(message, ("tm", "rows"), 0, 0, tiled=True)

    steps = columns // 2 // min(2, columns // 2)
    block = columns // steps
    rows_spec = pl.BlockSpec((2, block, time, outputs), lambda g: (0, g, 0, 0))
    return pl.pallas_call(
        functools.partial(norm_body, float(height * columns * time), outputs // GROUPS),
        grid=(steps,),
        out_shape=shape((height // 2, columns // 2, time, 4 * outputs), BF16),
        in_specs=[VMEM, VMEM, VMEM] + [rows_spec] * 4,
        out_specs=pl.BlockSpec((height // 2, block // 2, time, 4 * outputs), lambda g: (0, g, 0, 0)),
        scratch_shapes=[pltpu.VMEM((8, outputs), F32)],
        compiler_params=pltpu.CompilerParams(vmem_limit_bytes=40 * MIB),
    )(messages, norm_gain.reshape(-1, 128), norm_bias.reshape(-1, 128), done0, done1, done2, done3)


def solution(mesh):
    placed = (P("tm", "rows", None, None), P(), P(), P())
    return jax.shard_map(
        per_device,
        mesh=mesh,
        in_specs=placed,
        out_specs=P("rows", "tm", None, None),
        check_vma=False,
    )
```

```python
import functools

import jax
import jax.numpy as jnp
from jax import lax
from jax.experimental import pallas as pl
from jax.experimental.pallas import tpu as pltpu
from jax.sharding import PartitionSpec as P

GROUPS = 32
LEVELS = 3
TAPS = 3
inv_root = 0.7071067811865476
F32 = jnp.float32
BF16 = jnp.bfloat16
VMEM = pl.BlockSpec(memory_space=pltpu.VMEM)
SMEM = pl.BlockSpec(memory_space=pltpu.SMEM)
HBM = pl.BlockSpec(memory_space=pltpu.HBM)
MIB = 1 << 20
MARK = jax.ShapeDtypeStruct((8, 128), jnp.float32)


def shape(dims, dtype):
    return jax.ShapeDtypeStruct(dims, dtype)


def handing_on(body, inputs):
    def wrapped(me_ref, before, *refs):
        refs[inputs][...] = jnp.zeros_like(before)
        body(me_ref, *refs[:inputs], *refs[inputs + 1 :])

    return wrapped


def on_core(body, outs, scalar, arrays, scratch=(), limit=28, specs=None):
    mark, *given = pl.pallas_call(
        handing_on(body, len(arrays)),
        out_shape=[MARK] + outs,
        in_specs=[SMEM, VMEM] + (specs or [VMEM] * len(arrays)),
        out_specs=[VMEM] + [VMEM] * len(outs),
        scratch_shapes=list(scratch),
        compiler_params=pltpu.CompilerParams(vmem_limit_bytes=limit * MIB),
        cost_estimate=pl.CostEstimate(flops=0, bytes_accessed=0, transcendentals=0),
    )(*scalar, *arrays)
    return (scalar[0], mark), *given


def swap(block, mask):
    count = lax.axis_size("tm")
    return lax.ppermute(block, "tm", [(i, i ^ mask) for i in range(count)])


def combined(bits):
    masks = [0]
    for bit in bits:
        masks += [m | 1 << bit for m in masks]
    return masks[1:]


class Trip:
    def __init__(self, rows, groups):
        self.rows = rows
        self.groups = [g for g in groups if g]
        self.count = 1 << sum(len(g) for g in self.groups)
        self.place = {(0, m): None for m in range(self.count)}
        self.arrays = []
        self.steps = 0

    def leaving(self):
        group = sum(1 << b for b in self.groups[self.steps])
        past = sum(1 << b for g in self.groups[: self.steps] for b in g)
        held = sorted(k for k in self.place if not k[1] & past)
        return {m: [k for k in held if k[1] & group == m] for m in combined(self.groups[self.steps])}

    def swap(self, blocks):
        for (mask, wanted), block in zip(self.leaving().items(), blocks):
            got = lax.ppermute(block, "tm", [(i, i ^ mask) for i in range(self.count)])
            for i, (source, dest) in enumerate(wanted):
                self.place[(source ^ mask, dest ^ mask)] = (len(self.arrays), i)
            self.arrays.append(got)
        self.steps += 1

    def step(self, me, after=()):
        places = [[self.place[k] for k in wanted] for wanted in self.leaving().values()]

        def body(me_ref, *refs):
            for out, chosen in zip(refs[-len(places) :], places):
                for i, (array, at) in enumerate(chosen):
                    out[i] = refs[array][at]

        outs = [shape((len(p),) + self.arrays[0].shape[1:], BF16) for p in places]
        me, *blocks = on_core(body, outs, me, self.arrays + list(after), limit=24)
        self.swap(blocks)
        return me

    def gather(self, me, refs, blocks):
        for source in range(self.count):
            array, at = self.place[(source, 0)]
            blocks[me ^ source] = refs[array][at]


def part_body(trips, me_ref, video, *refs):
    *outs, wide = refs
    width = video.shape[2]
    columns = width // trips[0].count
    for i, trip in enumerate(trips):
        cells = jnp.swapaxes(jnp.concatenate([video[:, h] for h in trip.rows], 0), 0, 1)
        edge = jnp.zeros((1,) + cells.shape[1:], BF16)
        wide[0:1] = edge
        wide[1 : width + 1] = cells
        wide[width + 1 : width + 2] = edge
        for _, masks in trip.first:
            out = outs.pop(0)
            for place, mask in enumerate(masks):
                out[place] = wide[pl.ds((me_ref[0] ^ mask) * columns, columns + 2)]


def part_rows(me, video, trips):
    frames, _, width, channels = video.shape
    count = trips[0].count
    tail = (width // count + 2, 2 * frames, channels)
    outs = []
    for trip in trips:
        leaving = trip.leaving()
        away = [k[1] for wanted in leaving.values() for k in wanted]
        kept = [m for m in range(count) if m not in away]
        trip.first = [(0, kept)] + [(m, [k[1] for k in wanted]) for m, wanted in leaving.items()]
        trip.place.update({(0, m): (0, i) for i, m in enumerate(kept)})
        outs += [shape((len(masks),) + tail, BF16) for _, masks in trip.first]
    body = functools.partial(part_body, trips)
    scratch = [pltpu.VMEM((width + 2, 2 * frames, channels), BF16)]
    me, *parts = on_core(body, outs, me, [video], scratch, limit=24)
    for trip in trips:
        trip.arrays.append(parts.pop(0))
        trip.swap([parts.pop(0) for _ in trip.first[1:]])
    return me


def widen(wide, row, column, cells):
    channels = cells.shape[1]
    frame = lax.broadcasted_iota(jnp.int32, cells.shape, 0)
    for tap in range(TAPS):
        back = TAPS - 1 - tap
        moved = cells
        if back:
            moved = jnp.where(frame < back, 0.0, pltpu.roll(cells, back, 0))
        wide[row, column, :, tap * channels : (tap + 1) * channels] = moved.astype(BF16)


def wavelet_rows(blocks, wide, plain=None):
    count, columns = blocks.shape[:2]
    rows = wide.shape[0]
    frames = blocks.shape[2] // rows

    def column(i, _):
        values = [blocks[b, i].astype(F32) for b in range(count)]
        for level in range(LEVELS):
            span = 1 << level
            later = list(values)
            for b in range(count):
                if not b & span:
                    later[b] = (values[b] + values[b + span]) * inv_root
                    later[b + span] = (values[b] - values[b + span]) * inv_root
            values = later
        for row in range(rows):
            cells = jnp.concatenate([v[row * frames : (row + 1) * frames] for v in values], 0)
            widen(wide, row, i, cells)
            if plain is not None:
                plain[row, i] = cells.astype(BF16)
        return 0

    lax.fori_loop(0, columns, column, 0)


def outer_body(trip, me_ref, *refs):
    *held, wide, plain, blocks = refs
    trip.gather(me_ref[0], held, blocks)
    wavelet_rows(blocks, wide, plain)


def taps(w_ref, terms, before=None):
    columns = terms[0][0].shape[1] - 2
    left, right = [], []
    for wide, row, i in terms:
        for j in range(TAPS):
            cells = wide[row, pl.ds(j, columns)]
            left.append(cells.reshape(-1, cells.shape[-1]))
            right += [w_ref[k, i, j] for k in range(TAPS)]
    total = jnp.dot(
        jnp.concatenate(left, -1), jnp.concatenate(right, 0), preferred_element_type=F32
    )
    if before is not None:
        total = total + before
    return total


def row_sums(total):
    mean = jnp.sum(total, 0, keepdims=True) * (1.0 / total.shape[0])
    apart = total - mean
    return mean, jnp.sum(apart * apart, 0, keepdims=True)


def finish(total, out, sums, row):
    out[row] = total.reshape(out.shape[1:])
    mean, squares = row_sums(total)
    sums[row, 0:1] = mean
    sums[row, 1:2] = squares


def keep(total, out, row):
    out[row] = total.reshape(out.shape[1:])


def flat(ref, row):
    return ref[row].reshape(-1, ref.shape[-1])


def stage_a(trip, me_ref, w_ref, outer, *refs):
    *held, part0, part1, part2, wide, blocks = refs
    trip.gather(me_ref[0], held, blocks)
    wavelet_rows(blocks, wide)
    keep(taps(w_ref, [(outer, 0, 1), (wide, 0, 2)]), part0, 0)
    keep(taps(w_ref, [(wide, 1, 0), (outer, 1, 1)]), part0, 1)
    keep(taps(w_ref, [(outer, 0, 0), (wide, 0, 1)]), part1, 0)
    keep(taps(w_ref, [(wide, 1, 1), (outer, 1, 2)]), part1, 1)
    keep(taps(w_ref, [(wide, 0, 0)]), part2, 0)
    keep(taps(w_ref, [(wide, 1, 2)]), part2, 1)


def stage_b(trip, me_ref, w_ref, above, below, part0, part1, part2, *refs):
    *held, done0, done1, next2, part3, sums, wide, halo, blocks = refs
    trip.gather(me_ref[0], held, blocks)
    wavelet_rows(blocks, wide)

    def column(i, _):
        widen(halo, 0, i, above[i].astype(F32))
        widen(halo, 1, i, below[i].astype(F32))
        return 0

    lax.fori_loop(0, above.shape[0], column, 0)
    finish(taps(w_ref, [(wide, 0, 2)], flat(part1, 0)), done1, sums.at[2:4], 0)
    finish(taps(w_ref, [(wide, 1, 0)], flat(part1, 1)), done1, sums.at[2:4], 1)
    keep(taps(w_ref, [(wide, 0, 1)], flat(part2, 0)), next2, 0)
    keep(taps(w_ref, [(wide, 1, 1)], flat(part2, 1)), next2, 1)
    keep(taps(w_ref, [(wide, 0, 0)]), part3, 0)
    keep(taps(w_ref, [(wide, 1, 2)]), part3, 1)
    finish(taps(w_ref, [(halo, 0, 0)], flat(part0, 0)), done0, sums, 0)
    finish(taps(w_ref, [(halo, 1, 2)], flat(part0, 1)), done0, sums, 1)


def stage_c(trip, me_ref, w_ref, part2, part3, earlier, *refs):
    *held, done2, done3, message, sums, wide, blocks = refs
    trip.gather(me_ref[0], held, blocks)
    wavelet_rows(blocks, wide)
    finish(taps(w_ref, [(wide, 0, 2)], flat(part2, 0)), done2, sums, 0)
    finish(taps(w_ref, [(wide, 1, 0)], flat(part2, 1)), done2, sums, 1)
    finish(taps(w_ref, [(wide, 0, 1), (wide, 1, 2)], flat(part3, 0)), done3, sums.at[2:4], 0)
    finish(taps(w_ref, [(wide, 0, 0), (wide, 1, 1)], flat(part3, 1)), done3, sums.at[2:4], 1)
    rows = [sums[r] for r in range(4)]
    rows += [earlier[r] for r in range(4)]
    entries = wide.shape[2] * (wide.shape[1] - 2)
    mean = sum(r[0:1] for r in rows) * (1.0 / len(rows))
    squares = sum(r[1:2] + entries * (r[0:1] - mean) * (r[0:1] - mean) for r in rows)
    lanes = message.shape[-1]
    parts = [v[:, c : c + lanes] for v in (mean, squares) for c in range(0, mean.shape[1], lanes)]
    packed = jnp.concatenate(parts + [jnp.zeros((8 - len(parts), lanes), F32)], 0)
    message[...] = jnp.broadcast_to(packed[None], message.shape)


def over_group(values, size):
    lanes = values.shape[-1]
    lane = lax.broadcasted_iota(jnp.int32, values.shape, values.ndim - 1)
    step = 1
    while step < size:
        axis = values.ndim - 1
        down = pltpu.roll(values, step, axis)
        up = pltpu.roll(values, lanes - step, axis)
        values = values + jnp.where((lane & step) != 0, down, up)
        step *= 2
    return values


def norm_body(entries, size, all_ref, gain_ref, bias_ref, *refs):
    *rows, out, affine = refs

    @pl.when(pl.program_id(0) == 0)
    def _():
        devices = all_ref.shape[0]
        half = gain_ref.shape[0]
        means = all_ref[:, 0:half]
        mean = jnp.sum(means, 0) * (1.0 / devices)
        apart = means - mean[None]
        squares = jnp.sum(all_ref[:, half : 2 * half] + entries * apart * apart, 0)
        group_mean = over_group(mean, size) * (1.0 / size)
        apart = mean - group_mean
        group = over_group(squares + (entries * devices) * apart * apart, size)
        variance = group * (1.0 / (entries * devices * size))
        scale = (0.5 * gain_ref[...]) / jnp.sqrt(variance + 1e-05)
        for p in range(half):
            lanes = slice(p * scale.shape[1], (p + 1) * scale.shape[1])
            affine[0:1, lanes] = group_mean[p : p + 1]
            affine[1:2, lanes] = scale[p : p + 1]
            affine[2:3, lanes] = 0.5 * bias_ref[p : p + 1]

    mean, scale, bias = affine[0:1], affine[1:2], affine[2:3]
    channels = mean.shape[1]
    height = 2 * len(rows)
    for h in range(height):
        ref, place = (rows[h], 0) if h < len(rows) else (rows[height - 1 - h], 1)
        for w in range(ref.shape[1]):
            half_v = (ref[place, w] - mean) * scale + bias
            value = half_v + half_v * jnp.tanh(half_v)
            lanes = (h % 2 * 2 + w % 2) * channels
            out[h // 2, w // 2, :, lanes : lanes + channels] = value.astype(BF16)


def per_device(video, conv_weight, norm_gain, norm_bias):
    frames, height, width, channels = video.shape
    outputs = conv_weight.shape[-1]
    count = lax.axis_size("tm")
    strips = lax.axis_size("rows")
    devices = count * strips
    columns = width // count
    time = frames * count
    me = lax.axis_index("tm").astype(jnp.int32).reshape(1)
    me = (me, jnp.zeros(MARK.shape, MARK.dtype))
    bits = count.bit_length() - 1
    top, rest = bits - 1, list(range(1, bits - 1))
    outer_trip = Trip((0, 7), [[top], [0] + rest])
    third_trip = Trip((2, 5), [[0], [top], rest])
    second_trip = Trip((1, 6), [[0], rest, [top]])
    inner_trip = Trip((3, 4), [rest, [0], [top]])
    trips = [outer_trip, third_trip, second_trip, inner_trip]
    me = part_rows(me, video, trips)
    for trip in (outer_trip, third_trip, second_trip, inner_trip, third_trip, second_trip, inner_trip):
        me = trip.step(me)

    def blocks(rows):
        return pltpu.VMEM((count, columns + 2, rows * frames, channels), BF16)

    def wide(rows):
        return (rows, columns + 2, time, TAPS * channels)

    row_pair = shape((2, columns, time, outputs), F32)
    four_sums = shape((4, 2, outputs), F32)

    me, outer, plain = on_core(
        functools.partial(outer_body, outer_trip),
        [shape(wide(2), BF16), shape((2, columns + 2, time, channels), BF16)],
        me,
        outer_trip.arrays,
        [blocks(2)],
    )
    down = [(i, i + 1) for i in range(strips - 1)]
    up = [(i + 1, i) for i in range(strips - 1)]
    above = lax.ppermute(plain[1], "rows", down)
    below = lax.ppermute(plain[0], "rows", up)
    me, part0, part1, part2 = on_core(
        functools.partial(stage_a, second_trip),
        [row_pair, row_pair, row_pair],
        me,
        [conv_weight, outer] + second_trip.arrays,
        [pltpu.VMEM(wide(2), BF16), blocks(2)],
    )
    me, done0, done1, part2, part3, sums = on_core(
        functools.partial(stage_b, third_trip),
        [row_pair, row_pair, row_pair, row_pair, four_sums],
        me,
        [conv_weight, above, below, part0, part1, part2] + third_trip.arrays,
        [pltpu.VMEM(wide(2), BF16), pltpu.VMEM(wide(2), BF16), blocks(2)],
    )
    me, done2, done3, message = on_core(
        functools.partial(stage_c, inner_trip),
        [row_pair, row_pair, shape((devices, 8, 128), F32)],
        me,
        [conv_weight, part2, part3, sums] + inner_trip.arrays,
        [pltpu.VMEM((4, 2, outputs), F32), pltpu.VMEM(wide(2), BF16), blocks(2)],
    )
    messages = lax.all_to_all(message, ("tm", "rows"), 0, 0, tiled=True)

    steps = columns // 2 // min(2, columns // 2)
    block = columns // steps
    rows_spec = pl.BlockSpec((2, block, time, outputs), lambda g: (0, g, 0, 0))
    return pl.pallas_call(
        functools.partial(norm_body, float(height * columns * time), outputs // GROUPS),
        grid=(steps,),
        out_shape=shape((height // 2, columns // 2, time, 4 * outputs), BF16),
        in_specs=[VMEM, VMEM, VMEM] + [rows_spec] * 4,
        out_specs=pl.BlockSpec((height // 2, block // 2, time, 4 * outputs), lambda g: (0, g, 0, 0)),
        scratch_shapes=[pltpu.VMEM((8, outputs), F32)],
        compiler_params=pltpu.CompilerParams(vmem_limit_bytes=40 * MIB),
    )(messages, norm_gain.reshape(-1, 128), norm_bias.reshape(-1, 128), done0, done1, done2, done3)


def solution(mesh):
    placed = (P("tm", "rows", None, None), P(), P(), P())
    return jax.shard_map(
        per_device,
        mesh=mesh,
        in_specs=placed,
        out_specs=P("rows", "tm", None, None),
        check_vma=False,
    )
```

```python
import functools

import jax
import jax.numpy as jnp
from jax import lax
from jax.experimental import pallas as pl
from jax.experimental.pallas import tpu as pltpu
from jax.sharding import PartitionSpec as P

GROUPS = 32
LEVELS = 3
TAPS = 3
inv_root = 0.7071067811865476
F32 = jnp.float32
BF16 = jnp.bfloat16
VMEM = pl.BlockSpec(memory_space=pltpu.VMEM)
SMEM = pl.BlockSpec(memory_space=pltpu.SMEM)
HBM = pl.BlockSpec(memory_space=pltpu.HBM)
MIB = 1 << 20
MARK = jax.ShapeDtypeStruct((8, 128), jnp.float32)


def shape(dims, dtype):
    return jax.ShapeDtypeStruct(dims, dtype)


def handing_on(body, inputs):
    def wrapped(me_ref, before, *refs):
        refs[inputs][...] = jnp.zeros_like(before)
        body(me_ref, *refs[:inputs], *refs[inputs + 1 :])

    return wrapped


def on_core(body, outs, scalar, arrays, scratch=(), limit=28, specs=None):
    mark, *given = pl.pallas_call(
        handing_on(body, len(arrays)),
        out_shape=[MARK] + outs,
        in_specs=[SMEM, VMEM] + (specs or [VMEM] * len(arrays)),
        out_specs=[VMEM] + [VMEM] * len(outs),
        scratch_shapes=list(scratch),
        compiler_params=pltpu.CompilerParams(vmem_limit_bytes=limit * MIB),
        cost_estimate=pl.CostEstimate(flops=0, bytes_accessed=0, transcendentals=0),
    )(*scalar, *arrays)
    return (scalar[0], mark), *given


def swap(block, mask):
    count = lax.axis_size("tm")
    return lax.ppermute(block, "tm", [(i, i ^ mask) for i in range(count)])


def combined(bits):
    masks = [0]
    for bit in bits:
        masks += [m | 1 << bit for m in masks]
    return masks[:0:-1]


class Trip:
    def __init__(self, rows, groups):
        self.rows = rows
        self.groups = [g for g in groups if g]
        self.count = 1 << sum(len(g) for g in self.groups)
        self.place = {(0, m): None for m in range(self.count)}
        self.arrays = []
        self.steps = 0

    def leaving(self):
        group = sum(1 << b for b in self.groups[self.steps])
        past = sum(1 << b for g in self.groups[: self.steps] for b in g)
        held = sorted(k for k in self.place if not k[1] & past)
        return {m: [k for k in held if k[1] & group == m] for m in combined(self.groups[self.steps])}

    def swap(self, blocks):
        for (mask, wanted), block in zip(self.leaving().items(), blocks):
            got = lax.ppermute(block, "tm", [(i, i ^ mask) for i in range(self.count)])
            for i, (source, dest) in enumerate(wanted):
                self.place[(source ^ mask, dest ^ mask)] = (len(self.arrays), i)
            self.arrays.append(got)
        self.steps += 1

    def step(self, me, after=()):
        places = [[self.place[k] for k in wanted] for wanted in self.leaving().values()]

        def body(me_ref, *refs):
            for out, chosen in zip(refs[-len(places) :], places):
                for i, (array, at) in enumerate(chosen):
                    out[i] = refs[array][at]

        outs = [shape((len(p),) + self.arrays[0].shape[1:], BF16) for p in places]
        me, *blocks = on_core(body, outs, me, self.arrays + list(after), limit=24)
        self.swap(blocks)
        return me

    def gather(self, me, refs, blocks):
        for source in range(self.count):
            array, at = self.place[(source, 0)]
            blocks[me ^ source] = refs[array][at]


def part_body(trips, me_ref, video, *refs):
    *outs, wide = refs
    width = video.shape[2]
    columns = width // trips[0].count
    for i, trip in enumerate(trips):
        cells = jnp.swapaxes(jnp.concatenate([video[:, h] for h in trip.rows], 0), 0, 1)
        edge = jnp.zeros((1,) + cells.shape[1:], BF16)
        wide[0:1] = edge
        wide[1 : width + 1] = cells
        wide[width + 1 : width + 2] = edge
        for _, masks in trip.first:
            out = outs.pop(0)
            for place, mask in enumerate(masks):
                out[place] = wide[pl.ds((me_ref[0] ^ mask) * columns, columns + 2)]


def part_rows(me, video, trips):
    frames, _, width, channels = video.shape
    count = trips[0].count
    tail = (width // count + 2, 2 * frames, channels)
    outs = []
    for trip in trips:
        leaving = trip.leaving()
        away = [k[1] for wanted in leaving.values() for k in wanted]
        kept = [m for m in range(count) if m not in away]
        trip.first = [(0, kept)] + [(m, [k[1] for k in wanted]) for m, wanted in leaving.items()]
        trip.place.update({(0, m): (0, i) for i, m in enumerate(kept)})
        outs += [shape((len(masks),) + tail, BF16) for _, masks in trip.first]
    body = functools.partial(part_body, trips)
    scratch = [pltpu.VMEM((width + 2, 2 * frames, channels), BF16)]
    me, *parts = on_core(body, outs, me, [video], scratch, limit=24)
    for trip in trips:
        trip.arrays.append(parts.pop(0))
        trip.swap([parts.pop(0) for _ in trip.first[1:]])
    return me


def widen(wide, row, column, cells):
    channels = cells.shape[1]
    frame = lax.broadcasted_iota(jnp.int32, cells.shape, 0)
    for tap in range(TAPS):
        back = TAPS - 1 - tap
        moved = cells
        if back:
            moved = jnp.where(frame < back, 0.0, pltpu.roll(cells, back, 0))
        wide[row, column, :, tap * channels : (tap + 1) * channels] = moved.astype(BF16)


def wavelet_rows(blocks, wide, plain=None):
    count, columns = blocks.shape[:2]
    rows = wide.shape[0]
    frames = blocks.shape[2] // rows

    def column(i, _):
        values = [blocks[b, i].astype(F32) for b in range(count)]
        for level in range(LEVELS):
            span = 1 << level
            later = list(values)
            for b in range(count):
                if not b & span:
                    later[b] = (values[b] + values[b + span]) * inv_root
                    later[b + span] = (values[b] - values[b + span]) * inv_root
            values = later
        for row in range(rows):
            cells = jnp.concatenate([v[row * frames : (row + 1) * frames] for v in values], 0)
            widen(wide, row, i, cells)
            if plain is not None:
                plain[row, i] = cells.astype(BF16)
        return 0

    lax.fori_loop(0, columns, column, 0)


def outer_body(trip, me_ref, *refs):
    *held, wide, plain, blocks = refs
    trip.gather(me_ref[0], held, blocks)
    wavelet_rows(blocks, wide, plain)


def taps(w_ref, terms, before=None):
    columns = terms[0][0].shape[1] - 2
    left, right = [], []
    for wide, row, i in terms:
        for j in range(TAPS):
            cells = wide[row, pl.ds(j, columns)]
            left.append(cells.reshape(-1, cells.shape[-1]))
            right += [w_ref[k, i, j] for k in range(TAPS)]
    total = jnp.dot(
        jnp.concatenate(left, -1), jnp.concatenate(right, 0), preferred_element_type=F32
    )
    if before is not None:
        total = total + before
    return total


def row_sums(total):
    mean = jnp.sum(total, 0, keepdims=True) * (1.0 / total.shape[0])
    apart = total - mean
    return mean, jnp.sum(apart * apart, 0, keepdims=True)


def finish(total, out, sums, row):
    out[row] = total.reshape(out.shape[1:])
    mean, squares = row_sums(total)
    sums[row, 0:1] = mean
    sums[row, 1:2] = squares


def keep(total, out, row):
    out[row] = total.reshape(out.shape[1:])


def flat(ref, row):
    return ref[row].reshape(-1, ref.shape[-1])


def stage_o(me_ref, w_ref, outer, part0, part1):
    keep(taps(w_ref, [(outer, 0, 1)]), part0, 0)
    keep(taps(w_ref, [(outer, 1, 1)]), part0, 1)
    keep(taps(w_ref, [(outer, 0, 0)]), part1, 0)
    keep(taps(w_ref, [(outer, 1, 2)]), part1, 1)


def stage_a(trip, me_ref, w_ref, part1, *refs):
    *held, next1, part2, part3, wide, blocks = refs
    trip.gather(me_ref[0], held, blocks)
    wavelet_rows(blocks, wide)
    keep(taps(w_ref, [(wide, 0, 2)], flat(part1, 0)), next1, 0)
    keep(taps(w_ref, [(wide, 1, 0)], flat(part1, 1)), next1, 1)
    keep(taps(w_ref, [(wide, 0, 1)]), part2, 0)
    keep(taps(w_ref, [(wide, 1, 1)]), part2, 1)
    keep(taps(w_ref, [(wide, 0, 0)]), part3, 0)
    keep(taps(w_ref, [(wide, 1, 2)]), part3, 1)


def stage_b(trip, me_ref, w_ref, above, below, part0, part1, part2, *refs):
    *held, done0, done1, next2, sums, wide, halo, blocks = refs
    trip.gather(me_ref[0], held, blocks)
    wavelet_rows(blocks, wide)

    def column(i, _):
        widen(halo, 0, i, above[i].astype(F32))
        widen(halo, 1, i, below[i].astype(F32))
        return 0

    lax.fori_loop(0, above.shape[0], column, 0)
    finish(taps(w_ref, [(halo, 0, 0), (wide, 0, 2)], flat(part0, 0)), done0, sums, 0)
    finish(taps(w_ref, [(wide, 1, 0), (halo, 1, 2)], flat(part0, 1)), done0, sums, 1)
    finish(taps(w_ref, [(wide, 0, 1)], flat(part1, 0)), done1, sums.at[2:4], 0)
    finish(taps(w_ref, [(wide, 1, 1)], flat(part1, 1)), done1, sums.at[2:4], 1)
    keep(taps(w_ref, [(wide, 0, 0)], flat(part2, 0)), next2, 0)
    keep(taps(w_ref, [(wide, 1, 2)], flat(part2, 1)), next2, 1)


def over_group(values, size):
    lanes = values.shape[-1]
    lane = lax.broadcasted_iota(jnp.int32, values.shape, values.ndim - 1)
    step = 1
    while step < size:
        axis = values.ndim - 1
        down = pltpu.roll(values, step, axis)
        up = pltpu.roll(values, lanes - step, axis)
        values = values + jnp.where((lane & step) != 0, down, up)
        step *= 2
    return values


def stage_c(trip, me_ref, w_ref, part2, part3, earlier, *refs):
    *held, done2, done3, message, sums, wide, blocks = refs
    trip.gather(me_ref[0], held, blocks)
    wavelet_rows(blocks, wide)
    finish(taps(w_ref, [(wide, 0, 2)], flat(part2, 0)), done2, sums, 0)
    finish(taps(w_ref, [(wide, 1, 0)], flat(part2, 1)), done2, sums, 1)
    finish(taps(w_ref, [(wide, 0, 1), (wide, 1, 2)], flat(part3, 0)), done3, sums.at[2:4], 0)
    finish(taps(w_ref, [(wide, 0, 0), (wide, 1, 1)], flat(part3, 1)), done3, sums.at[2:4], 1)
    rows = [sums[r] for r in range(4)]
    rows += [earlier[r] for r in range(4)]
    entries = wide.shape[2] * (wide.shape[1] - 2)
    mean = sum(r[0:1] for r in rows) * (1.0 / len(rows))
    squares = sum(r[1:2] + entries * (r[0:1] - mean) * (r[0:1] - mean) for r in rows)
    lanes = message.shape[-1]
    halves = range(0, mean.shape[1], lanes)
    mean = jnp.concatenate([mean[:, c : c + lanes] for c in halves], 0)
    squares = jnp.concatenate([squares[:, c : c + lanes] for c in halves], 0)
    size = mean.size // GROUPS
    group_mean = over_group(mean, size) * (1.0 / size)
    apart = mean - group_mean
    group = over_group(squares + (entries * len(rows)) * apart * apart, size)
    slot = lax.broadcasted_iota(jnp.int32, (1, lanes), 1) % size
    packed = jnp.zeros((1, lanes), F32)
    for i, value in enumerate([group_mean[0:1], group_mean[1:2], group[0:1], group[1:2]]):
        packed = jnp.where(slot == i, value, packed)
    message[...] = jnp.broadcast_to(packed[None], message.shape)


def norm_body(entries, size, all_ref, gain_ref, bias_ref, *refs):
    *rows, out, affine = refs

    @pl.when(pl.program_id(0) == 0)
    def _():
        devices = all_ref.shape[0]
        given = all_ref[:, 0]
        half = gain_ref.shape[0]
        total = jnp.sum(given, 0, keepdims=True)
        apart = given - total * (1.0 / devices)
        spread = jnp.sum(apart * apart, 0, keepdims=True)
        slot = lax.broadcasted_iota(jnp.int32, total.shape, 1) % size

        def of(values, i):
            return over_group(jnp.where(slot == i, values, 0.0), size)

        group_mean = jnp.concatenate([of(total, p) for p in range(half)], 0) * (1.0 / devices)
        squares = [of(total, half + p) + (entries * size) * of(spread, p) for p in range(half)]
        variance = jnp.concatenate(squares, 0) * (1.0 / (entries * devices * size))
        scale = (0.5 * gain_ref[...]) / jnp.sqrt(variance + 1e-05)
        for p in range(half):
            lanes = slice(p * scale.shape[1], (p + 1) * scale.shape[1])
            affine[0:1, lanes] = group_mean[p : p + 1]
            affine[1:2, lanes] = scale[p : p + 1]
            affine[2:3, lanes] = 0.5 * bias_ref[p : p + 1]

    mean, scale, bias = affine[0:1], affine[1:2], affine[2:3]
    channels = mean.shape[1]
    height = 2 * len(rows)
    for h in range(height):
        ref, place = (rows[h], 0) if h < len(rows) else (rows[height - 1 - h], 1)
        for w in range(2 * out.shape[1]):
            half_v = (ref[place, pl.program_id(0) * (2 * out.shape[1]) + w] - mean) * scale + bias
            value = half_v + half_v * jnp.tanh(half_v)
            lanes = (h % 2 * 2 + w % 2) * channels
            out[h // 2, w // 2, :, lanes : lanes + channels] = value.astype(BF16)


def per_device(video, conv_weight, norm_gain, norm_bias):
    frames, height, width, channels = video.shape
    outputs = conv_weight.shape[-1]
    count = lax.axis_size("tm")
    strips = lax.axis_size("rows")
    devices = count * strips
    columns = width // count
    time = frames * count
    me = lax.axis_index("tm").astype(jnp.int32).reshape(1)
    me = (me, jnp.zeros(MARK.shape, MARK.dtype))
    bits = count.bit_length() - 1
    top, rest = bits - 1, list(range(1, bits - 1))
    outer_trip = Trip((0, 7), [[top], [0] + rest])
    third_trip = Trip((2, 5), [[0], [top], rest])
    second_trip = Trip((1, 6), [rest, [0], [top]])
    inner_trip = Trip((3, 4), [[0], rest + [top]])
    trips = [outer_trip, third_trip, second_trip, inner_trip]
    me = part_rows(me, video, trips)
    for trip in (outer_trip, third_trip, second_trip, third_trip, second_trip):
        me = trip.step(me)

    def blocks(rows):
        return pltpu.VMEM((count, columns + 2, rows * frames, channels), BF16)

    def wide(rows):
        return (rows, columns + 2, time, TAPS * channels)

    row_pair = shape((2, columns, time, outputs), F32)
    four_sums = shape((4, 2, outputs), F32)

    me, outer, plain = on_core(
        functools.partial(outer_body, outer_trip),
        [shape(wide(2), BF16), shape((2, columns + 2, time, channels), BF16)],
        me,
        outer_trip.arrays,
        [blocks(2)],
    )
    down = [(i, i + 1) for i in range(strips - 1)]
    up = [(i + 1, i) for i in range(strips - 1)]
    above = lax.ppermute(plain[1], "rows", down)
    below = lax.ppermute(plain[0], "rows", up)
    me, part0, part1 = on_core(stage_o, [row_pair, row_pair], me, [conv_weight, outer])
    me = inner_trip.step(me)
    me, part1, part2, part3 = on_core(
        functools.partial(stage_a, third_trip),
        [row_pair, row_pair, row_pair],
        me,
        [conv_weight, part1] + third_trip.arrays,
        [pltpu.VMEM(wide(2), BF16), blocks(2)],
    )
    me, done0, done1, part2, sums = on_core(
        functools.partial(stage_b, second_trip),
        [row_pair, row_pair, row_pair, four_sums],
        me,
        [conv_weight, above, below, part0, part1, part2] + second_trip.arrays,
        [pltpu.VMEM(wide(2), BF16), pltpu.VMEM(wide(2), BF16), blocks(2)],
    )
    me, done2, done3, message = on_core(
        functools.partial(stage_c, inner_trip),
        [row_pair, row_pair, shape((devices, 1, 128), F32)],
        me,
        [conv_weight, part2, part3, sums] + inner_trip.arrays,
        [pltpu.VMEM((4, 2, outputs), F32), pltpu.VMEM(wide(2), BF16), blocks(2)],
    )
    messages = lax.all_to_all(message, ("tm", "rows"), 0, 0, tiled=True)

    steps = columns // 2 // min(2, columns // 2)
    block = columns // steps
    return pl.pallas_call(
        functools.partial(norm_body, float(height * columns * time), outputs // GROUPS),
        grid=(steps,),
        out_shape=shape((height // 2, columns // 2, time, 4 * outputs), BF16),
        in_specs=[VMEM] * 7,
        out_specs=pl.BlockSpec((height // 2, block // 2, time, 4 * outputs), lambda g: (0, g, 0, 0)),
        scratch_shapes=[pltpu.VMEM((8, outputs), F32)],
        compiler_params=pltpu.CompilerParams(vmem_limit_bytes=40 * MIB),
    )(messages, norm_gain.reshape(-1, 128), norm_bias.reshape(-1, 128), done0, done1, done2, done3)


def solution(mesh):
    placed = (P("tm", "rows", None, None), P(), P(), P())
    return jax.shard_map(
        per_device,
        mesh=mesh,
        in_specs=placed,
        out_specs=P("rows", "tm", None, None),
        check_vma=False,
    )
```

```python
import functools

import jax
import jax.numpy as jnp
from jax import lax
from jax.experimental import pallas as pl
from jax.experimental.pallas import tpu as pltpu
from jax.sharding import PartitionSpec as P

GROUPS = 32
LEVELS = 3
TAPS = 3
inv_root = 0.7071067811865476
F32 = jnp.float32
BF16 = jnp.bfloat16
VMEM = pl.BlockSpec(memory_space=pltpu.VMEM)
SMEM = pl.BlockSpec(memory_space=pltpu.SMEM)
HBM = pl.BlockSpec(memory_space=pltpu.HBM)
MIB = 1 << 20
MARK = jax.ShapeDtypeStruct((8, 128), jnp.float32)


def shape(dims, dtype):
    return jax.ShapeDtypeStruct(dims, dtype)


def handing_on(body, inputs):
    def wrapped(me_ref, before, *refs):
        refs[inputs][...] = jnp.zeros_like(before)
        body(me_ref, *refs[:inputs], *refs[inputs + 1 :])

    return wrapped


def on_core(body, outs, scalar, arrays, scratch=(), limit=28, specs=None, flops=0):
    mark, *given = pl.pallas_call(
        handing_on(body, len(arrays)),
        out_shape=[MARK] + outs,
        in_specs=[SMEM, VMEM] + (specs or [VMEM] * len(arrays)),
        out_specs=[VMEM] + [VMEM] * len(outs),
        scratch_shapes=list(scratch),
        compiler_params=pltpu.CompilerParams(vmem_limit_bytes=limit * MIB),
        cost_estimate=pl.CostEstimate(flops=flops, bytes_accessed=0, transcendentals=0),
    )(*scalar, *arrays)
    return (scalar[0], mark), *given


def swap(block, mask):
    count = lax.axis_size("tm")
    return lax.ppermute(block, "tm", [(i, i ^ mask) for i in range(count)])


def combined(bits):
    masks = [0]
    for bit in bits:
        masks += [m | 1 << bit for m in masks]
    return masks[:0:-1]


class Trip:
    def __init__(self, rows, groups, joined=False):
        self.rows, self.joined = rows, joined
        self.groups = [g for g in groups if g]
        self.count = 1 << sum(len(g) for g in self.groups)
        self.place = {(0, m): None for m in range(self.count)}
        self.arrays = []
        self.steps = 0

    def leaving(self):
        group = sum(1 << b for b in self.groups[self.steps])
        past = sum(1 << b for g in self.groups[: self.steps] for b in g)
        held = sorted(k for k in self.place if not k[1] & past)
        return {m: [k for k in held if k[1] & group == m] for m in combined(self.groups[self.steps])}

    def swap(self, blocks):
        for (mask, wanted), block in zip(self.leaving().items(), blocks):
            got = lax.ppermute(block, "tm", [(i, i ^ mask) for i in range(self.count)])
            for i, (source, dest) in enumerate(wanted):
                slab = self.joined and not self.steps
                self.place[(source ^ mask, dest ^ mask)] = (len(self.arrays), (dest ^ mask,) if slab else i)
            self.arrays.append(got)
        self.steps += 1

    def step(self, me, flops=0):
        places = [[self.place[k] for k in wanted] for wanted in self.leaving().values()]

        def body(me_ref, *refs):
            for out, chosen in zip(refs[-len(places) :], places):
                for i, (array, at) in enumerate(chosen):
                    out[i] = self.window(me_ref[0], refs[array], at)

        outs = [shape((len(p),) + self.arrays[0].shape[1:], BF16) for p in places]
        me, *blocks = on_core(body, outs, me, self.arrays, limit=24, flops=flops)
        self.swap(blocks)
        return me

    def gather(self, me, refs, blocks):
        for source in range(self.count):
            array, at = self.place[(source, 0)]
            blocks[me ^ source] = self.window(me, refs[array], at)

    def window(self, me, ref, at):
        if not isinstance(at, tuple):
            return ref[at]
        half = self.count // 2
        columns = (ref.shape[0] - 2) // half
        return ref[pl.ds(((me ^ at[0]) & (half - 1)) * columns, columns + 2)]


def part_body(trips, places, me_ref, video, *refs):
    *outs, wide = refs
    width = video.shape[2]
    columns = width // trips[0].count
    for i, trip in enumerate(trips):
        cells = jnp.swapaxes(jnp.concatenate([video[:, h] for h in places[i]], 0), 0, 1)
        edge = jnp.zeros((1,) + cells.shape[1:], BF16)
        wide[0:1] = edge
        wide[1 : width + 1] = cells
        wide[width + 1 : width + 2] = edge
        for mask, masks in trip.first:
            out = outs.pop(0)
            if mask and trip.joined:
                other = 1 - (me_ref[0] & mask) // mask
                out[...] = wide[pl.ds(other * (width // 2), width // 2 + 2)]
                continue
            for place, mask in enumerate(masks):
                out[place] = wide[pl.ds((me_ref[0] ^ mask) * columns, columns + 2)]


def part_rows(me, video, trips):
    frames, _, width, channels = video.shape
    count = trips[0].count
    tail = (width // count + 2, 2 * frames, channels)
    outs = []
    for trip in trips:
        leaving = trip.leaving()
        away = [k[1] for wanted in leaving.values() for k in wanted]
        kept = [m for m in range(count) if m not in away]
        trip.first = [(0, kept)] + [(m, [k[1] for k in wanted]) for m, wanted in leaving.items()]
        trip.place.update({(0, m): (0, i) for i, m in enumerate(kept)})
        slab = (width // 2 + 2,) + tail[1:]
        outs += [shape(slab if m and trip.joined else (len(masks),) + tail, BF16) for m, masks in trip.first]
    places = [trip.rows for trip in trips]
    if len(trips) == 1:
        video = jnp.concatenate([video[:, h : h + 1] for h in trips[0].rows], 1)
        places = [(0, 1)]
    body = functools.partial(part_body, trips, places)
    scratch = [pltpu.VMEM((width + 2, 2 * frames, channels), BF16)]
    me, *parts = on_core(body, outs, me, [video], scratch, limit=24)
    for trip in trips:
        trip.arrays.append(parts.pop(0))
        trip.swap([parts.pop(0) for _ in trip.first[1:]])
    return me


def widen(wide, row, column, cells):
    channels = cells.shape[1]
    frame = lax.broadcasted_iota(jnp.int32, cells.shape, 0)
    for tap in range(TAPS):
        back = TAPS - 1 - tap
        moved = cells
        if back:
            moved = jnp.where(frame < back, 0.0, pltpu.roll(cells, back, 0))
        wide[row, column, :, tap * channels : (tap + 1) * channels] = moved.astype(BF16)


def wavelet_rows(blocks, wide, plain=None):
    count, columns = blocks.shape[:2]
    rows = wide.shape[0]
    frames = blocks.shape[2] // rows

    def column(i, _):
        values = [blocks[b, i].astype(F32) for b in range(count)]
        for level in range(LEVELS):
            span = 1 << level
            later = list(values)
            for b in range(count):
                if not b & span:
                    later[b] = (values[b] + values[b + span]) * inv_root
                    later[b + span] = (values[b] - values[b + span]) * inv_root
            values = later
        for row in range(rows):
            cells = jnp.concatenate([v[row * frames : (row + 1) * frames] for v in values], 0)
            widen(wide, row, i, cells)
            if plain is not None:
                plain[row, i] = cells.astype(BF16)
        return 0

    lax.fori_loop(0, columns, column, 0)


def outer_body(trip, me_ref, *refs):
    *held, wide, plain, blocks = refs
    trip.gather(me_ref[0], held, blocks)
    wavelet_rows(blocks, wide, plain)


def taps(w_ref, terms, before=None):
    columns = terms[0][0].shape[1] - 2
    left, right = [], []
    for wide, row, i in terms:
        for j in range(TAPS):
            cells = wide[row, pl.ds(j, columns)]
            left.append(cells.reshape(-1, cells.shape[-1]))
            right += [w_ref[k, i, j] for k in range(TAPS)]
    total = jnp.dot(
        jnp.concatenate(left, -1), jnp.concatenate(right, 0), preferred_element_type=F32
    )
    if before is not None:
        total = total + before
    return total


def row_sums(total):
    mean = jnp.sum(total, 0, keepdims=True) * (1.0 / total.shape[0])
    apart = total - mean
    return mean, jnp.sum(apart * apart, 0, keepdims=True)


def finish(total, out, sums, row):
    out[row] = total.reshape(out.shape[1:])
    mean, squares = row_sums(total)
    sums[row, 0:1] = mean
    sums[row, 1:2] = squares


def keep(total, out, row):
    out[row] = total.reshape(out.shape[1:])


def flat(ref, row):
    return ref[row].reshape(-1, ref.shape[-1])


def stage_o(me_ref, w_ref, outer, part0, part1):
    keep(taps(w_ref, [(outer, 0, 1)]), part0, 0)
    keep(taps(w_ref, [(outer, 1, 1)]), part0, 1)
    keep(taps(w_ref, [(outer, 0, 0)]), part1, 0)
    keep(taps(w_ref, [(outer, 1, 2)]), part1, 1)


def stage_a(trip, me_ref, w_ref, part1, *refs):
    *held, next1, part2, part3, wide, blocks = refs
    trip.gather(me_ref[0], held, blocks)
    wavelet_rows(blocks, wide)
    keep(taps(w_ref, [(wide, 0, 2)], flat(part1, 0)), next1, 0)
    keep(taps(w_ref, [(wide, 1, 0)], flat(part1, 1)), next1, 1)
    keep(taps(w_ref, [(wide, 0, 1)]), part2, 0)
    keep(taps(w_ref, [(wide, 1, 1)]), part2, 1)
    keep(taps(w_ref, [(wide, 0, 0)]), part3, 0)
    keep(taps(w_ref, [(wide, 1, 2)]), part3, 1)


def stage_b(trip, me_ref, w_ref, above, below, part0, part1, part2, *refs):
    *held, done0, done1, next2, sums, wide, halo, blocks = refs
    trip.gather(me_ref[0], held, blocks)
    wavelet_rows(blocks, wide)

    def column(i, _):
        widen(halo, 0, i, above[i].astype(F32))
        widen(halo, 1, i, below[i].astype(F32))
        return 0

    lax.fori_loop(0, above.shape[0], column, 0)
    finish(taps(w_ref, [(halo, 0, 0), (wide, 0, 2)], flat(part0, 0)), done0, sums, 0)
    finish(taps(w_ref, [(wide, 1, 0), (halo, 1, 2)], flat(part0, 1)), done0, sums, 1)
    finish(taps(w_ref, [(wide, 0, 1)], flat(part1, 0)), done1, sums.at[2:4], 0)
    finish(taps(w_ref, [(wide, 1, 1)], flat(part1, 1)), done1, sums.at[2:4], 1)
    keep(taps(w_ref, [(wide, 0, 0)], flat(part2, 0)), next2, 0)
    keep(taps(w_ref, [(wide, 1, 2)], flat(part2, 1)), next2, 1)


def over_group(values, size):
    lanes = values.shape[-1]
    lane = lax.broadcasted_iota(jnp.int32, values.shape, values.ndim - 1)
    step = 1
    while step < size:
        axis = values.ndim - 1
        down = pltpu.roll(values, step, axis)
        up = pltpu.roll(values, lanes - step, axis)
        values = values + jnp.where((lane & step) != 0, down, up)
        step *= 2
    return values


def stage_c(trip, me_ref, w_ref, part2, part3, earlier, *refs):
    *held, done2, done3, message, sums, wide, blocks = refs
    trip.gather(me_ref[0], held, blocks)
    wavelet_rows(blocks, wide)
    finish(taps(w_ref, [(wide, 0, 2)], flat(part2, 0)), done2, sums, 0)
    finish(taps(w_ref, [(wide, 1, 0)], flat(part2, 1)), done2, sums, 1)
    finish(taps(w_ref, [(wide, 0, 1), (wide, 1, 2)], flat(part3, 0)), done3, sums.at[2:4], 0)
    finish(taps(w_ref, [(wide, 0, 0), (wide, 1, 1)], flat(part3, 1)), done3, sums.at[2:4], 1)
    rows = [sums[r] for r in range(4)]
    rows += [earlier[r] for r in range(4)]
    entries = wide.shape[2] * (wide.shape[1] - 2)
    mean = sum(r[0:1] for r in rows) * (1.0 / len(rows))
    squares = sum(r[1:2] + entries * (r[0:1] - mean) * (r[0:1] - mean) for r in rows)
    lanes = message.shape[-1]
    halves = range(0, mean.shape[1], lanes)
    mean = jnp.concatenate([mean[:, c : c + lanes] for c in halves], 0)
    squares = jnp.concatenate([squares[:, c : c + lanes] for c in halves], 0)
    size = mean.size // GROUPS
    group_mean = over_group(mean, size) * (1.0 / size)
    apart = mean - group_mean
    group = over_group(squares + (entries * len(rows)) * apart * apart, size)
    slot = lax.broadcasted_iota(jnp.int32, (1, lanes), 1) % size
    packed = jnp.zeros((1, lanes), F32)
    for i, value in enumerate([group_mean[0:1], group_mean[1:2], group[0:1], group[1:2]]):
        packed = jnp.where(slot == i, value, packed)
    message[...] = jnp.broadcast_to(packed[None], message.shape)


def norm_body(entries, size, all_ref, gain_ref, bias_ref, *refs):
    *rows, out, affine = refs

    @pl.when(pl.program_id(0) == 0)
    def _():
        devices = all_ref.shape[0]
        given = all_ref[:, 0]
        half = gain_ref.shape[0]
        total = jnp.sum(given, 0, keepdims=True)
        apart = given - total * (1.0 / devices)
        spread = jnp.sum(apart * apart, 0, keepdims=True)
        slot = lax.broadcasted_iota(jnp.int32, total.shape, 1) % size

        def of(values, i):
            return over_group(jnp.where(slot == i, values, 0.0), size)

        group_mean = jnp.concatenate([of(total, p) for p in range(half)], 0) * (1.0 / devices)
        squares = [of(total, half + p) + (entries * size) * of(spread, p) for p in range(half)]
        variance = jnp.concatenate(squares, 0) * (1.0 / (entries * devices * size))
        scale = (0.5 * gain_ref[...]) / jnp.sqrt(variance + 1e-05)
        for p in range(half):
            lanes = slice(p * scale.shape[1], (p + 1) * scale.shape[1])
            affine[0:1, lanes] = group_mean[p : p + 1]
            affine[1:2, lanes] = scale[p : p + 1]
            affine[2:3, lanes] = 0.5 * bias_ref[p : p + 1]

    mean, scale, bias = affine[0:1], affine[1:2], affine[2:3]
    channels = mean.shape[1]
    height = 2 * len(rows)
    for h in range(height):
        ref, place = (rows[h], 0) if h < len(rows) else (rows[height - 1 - h], 1)
        for w in range(2 * out.shape[1]):
            half_v = (ref[place, pl.program_id(0) * (2 * out.shape[1]) + w] - mean) * scale + bias
            value = half_v + half_v * jnp.tanh(half_v)
            lanes = (h % 2 * 2 + w % 2) * channels
            out[h // 2, w // 2, :, lanes : lanes + channels] = value.astype(BF16)


def per_device(video, conv_weight, norm_gain, norm_bias):
    frames, height, width, channels = video.shape
    outputs = conv_weight.shape[-1]
    count = lax.axis_size("tm")
    strips = lax.axis_size("rows")
    devices = count * strips
    columns = width // count
    time = frames * count
    me = lax.axis_index("tm").astype(jnp.int32).reshape(1)
    me = (me, jnp.zeros(MARK.shape, MARK.dtype))
    bits = count.bit_length() - 1
    top, rest = bits - 1, list(range(1, bits - 1))
    outer_trip = Trip((0, 7), [[top], [0] + rest], joined=True)
    third_trip = Trip((2, 5), [[0], [top], rest])
    second_trip = Trip((1, 6), [rest, [0], [top]])
    inner_trip = Trip((3, 4), [[0], rest + [top]])
    trips = [outer_trip, third_trip, second_trip, inner_trip]
    me = part_rows(me, video, trips[:1])
    me = part_rows(me, video, trips[1:])
    me = outer_trip.step(me, flops=3 * 10**9)
    for trip in (third_trip, second_trip, third_trip, second_trip):
        me = trip.step(me)

    def blocks(rows):
        return pltpu.VMEM((count, columns + 2, rows * frames, channels), BF16)

    def wide(rows):
        return (rows, columns + 2, time, TAPS * channels)

    row_pair = shape((2, columns, time, outputs), F32)
    four_sums = shape((4, 2, outputs), F32)

    me, outer, plain = on_core(
        functools.partial(outer_body, outer_trip),
        [shape(wide(2), BF16), shape((2, columns + 2, time, channels), BF16)],
        me,
        outer_trip.arrays,
        [blocks(2)],
    )
    down = [(i, i + 1) for i in range(strips - 1)]
    up = [(i + 1, i) for i in range(strips - 1)]
    above = lax.ppermute(plain[1], "rows", down)
    below = lax.ppermute(plain[0], "rows", up)
    me, part0, part1 = on_core(stage_o, [row_pair, row_pair], me, [conv_weight, outer])
    me = inner_trip.step(me)
    me, part1, part2, part3 = on_core(
        functools.partial(stage_a, third_trip),
        [row_pair, row_pair, row_pair],
        me,
        [conv_weight, part1] + third_trip.arrays,
        [pltpu.VMEM(wide(2), BF16), blocks(2)],
    )
    me, done0, done1, part2, sums = on_core(
        functools.partial(stage_b, second_trip),
        [row_pair, row_pair, row_pair, four_sums],
        me,
        [conv_weight, above, below, part0, part1, part2] + second_trip.arrays,
        [pltpu.VMEM(wide(2), BF16), pltpu.VMEM(wide(2), BF16), blocks(2)],
    )
    me, done2, done3, message = on_core(
        functools.partial(stage_c, inner_trip),
        [row_pair, row_pair, shape((devices, 1, 128), F32)],
        me,
        [conv_weight, part2, part3, sums] + inner_trip.arrays,
        [pltpu.VMEM((4, 2, outputs), F32), pltpu.VMEM(wide(2), BF16), blocks(2)],
    )
    messages = lax.all_to_all(message, ("tm", "rows"), 0, 0, tiled=True)

    steps = columns // 2 // min(2, columns // 2)
    block = columns // steps
    return pl.pallas_call(
        functools.partial(norm_body, float(height * columns * time), outputs // GROUPS),
        grid=(steps,),
        out_shape=shape((height // 2, columns // 2, time, 4 * outputs), BF16),
        in_specs=[VMEM] * 7,
        out_specs=pl.BlockSpec((height // 2, block // 2, time, 4 * outputs), lambda g: (0, g, 0, 0)),
        scratch_shapes=[pltpu.VMEM((8, outputs), F32)],
        compiler_params=pltpu.CompilerParams(vmem_limit_bytes=40 * MIB),
    )(messages, norm_gain.reshape(-1, 128), norm_bias.reshape(-1, 128), done0, done1, done2, done3)


def solution(mesh):
    placed = (P("tm", "rows", None, None), P(), P(), P())
    return jax.shard_map(
        per_device,
        mesh=mesh,
        in_specs=placed,
        out_specs=P("rows", "tm", None, None),
        check_vma=False,
    )
```

```python
import functools

import jax
import jax.numpy as jnp
from jax import lax
from jax.experimental import pallas as pl
from jax.experimental.pallas import tpu as pltpu
from jax.sharding import PartitionSpec as P

GROUPS = 32
LEVELS = 3
TAPS = 3
inv_root = 0.7071067811865476
F32 = jnp.float32
BF16 = jnp.bfloat16
VMEM = pl.BlockSpec(memory_space=pltpu.VMEM)
SMEM = pl.BlockSpec(memory_space=pltpu.SMEM)
HBM = pl.BlockSpec(memory_space=pltpu.HBM)
MIB = 1 << 20
MARK = jax.ShapeDtypeStruct((8, 128), jnp.float32)


def shape(dims, dtype):
    return jax.ShapeDtypeStruct(dims, dtype)


def handing_on(body, inputs):
    def wrapped(me_ref, before, *refs):
        refs[inputs][...] = jnp.zeros_like(before)
        body(me_ref, *refs[:inputs], *refs[inputs + 1 :])

    return wrapped


def on_core(body, outs, scalar, arrays, scratch=(), limit=28, specs=None, flops=0):
    mark, *given = pl.pallas_call(
        handing_on(body, len(arrays)),
        out_shape=[MARK] + outs,
        in_specs=[SMEM, VMEM] + (specs or [VMEM] * len(arrays)),
        out_specs=[VMEM] + [VMEM] * len(outs),
        scratch_shapes=list(scratch),
        compiler_params=pltpu.CompilerParams(vmem_limit_bytes=limit * MIB),
        cost_estimate=pl.CostEstimate(flops=flops, bytes_accessed=0, transcendentals=0),
    )(*scalar, *arrays)
    return (scalar[0], mark), *given


def swap(block, mask):
    count = lax.axis_size("tm")
    return lax.ppermute(block, "tm", [(i, i ^ mask) for i in range(count)])


def combined(bits):
    masks = [0]
    for bit in bits:
        masks += [m | 1 << bit for m in masks]
    return masks[:0:-1]


class Trip:
    def __init__(self, rows, groups, joined=False):
        self.rows, self.joined = rows, joined
        self.groups = [g for g in groups if g]
        self.count = 1 << sum(len(g) for g in self.groups)
        self.place = {(0, m): None for m in range(self.count)}
        self.arrays = []
        self.steps = 0

    def leaving(self):
        group = sum(1 << b for b in self.groups[self.steps])
        past = sum(1 << b for g in self.groups[: self.steps] for b in g)
        held = sorted(k for k in self.place if not k[1] & past)
        return {m: [k for k in held if k[1] & group == m] for m in combined(self.groups[self.steps])}

    def swap(self, blocks):
        for (mask, wanted), block in zip(self.leaving().items(), blocks):
            got = lax.ppermute(block, "tm", [(i, i ^ mask) for i in range(self.count)])
            for i, (source, dest) in enumerate(wanted):
                slab = self.joined and not self.steps
                self.place[(source ^ mask, dest ^ mask)] = (len(self.arrays), (dest ^ mask,) if slab else i)
            self.arrays.append(got)
        self.steps += 1

    def step(self, me, flops=0, after=()):
        places = [[self.place[k] for k in wanted] for wanted in self.leaving().values()]

        def body(me_ref, *refs):
            for out, chosen in zip(refs[-len(places) :], places):
                for i, (array, at) in enumerate(chosen):
                    out[i] = self.window(me_ref[0], refs[array], at)

        outs = [shape((len(p),) + self.arrays[0].shape[1:], BF16) for p in places]
        me, *blocks = on_core(body, outs, me, self.arrays + list(after), limit=24, flops=flops)
        self.swap(blocks)
        return me

    def gather(self, me, refs, blocks):
        for source in range(self.count):
            array, at = self.place[(source, 0)]
            blocks[me ^ source] = self.window(me, refs[array], at)

    def window(self, me, ref, at):
        if not isinstance(at, tuple):
            return ref[at]
        half = self.count // 2
        columns = (ref.shape[0] - 2) // half
        return ref[pl.ds(((me ^ at[0]) & (half - 1)) * columns, columns + 2)]


def part_body(trips, places, me_ref, video, *refs):
    *outs, wide = refs
    width = video.shape[2]
    columns = width // trips[0].count
    for i, trip in enumerate(trips):
        cells = jnp.swapaxes(jnp.concatenate([video[:, h] for h in places[i]], 0), 0, 1)
        edge = jnp.zeros((1,) + cells.shape[1:], BF16)
        wide[0:1] = edge
        wide[1 : width + 1] = cells
        wide[width + 1 : width + 2] = edge
        for mask, masks in trip.first:
            out = outs.pop(0)
            if mask and trip.joined:
                other = 1 - (me_ref[0] & mask) // mask
                out[...] = wide[pl.ds(other * (width // 2), width // 2 + 2)]
                continue
            for place, mask in enumerate(masks):
                out[place] = wide[pl.ds((me_ref[0] ^ mask) * columns, columns + 2)]


def part_rows(me, video, trips):
    frames, _, width, channels = video.shape
    count = trips[0].count
    tail = (width // count + 2, 2 * frames, channels)
    outs = []
    for trip in trips:
        leaving = trip.leaving()
        away = [k[1] for wanted in leaving.values() for k in wanted]
        kept = [m for m in range(count) if m not in away]
        trip.first = [(0, kept)] + [(m, [k[1] for k in wanted]) for m, wanted in leaving.items()]
        trip.place.update({(0, m): (0, i) for i, m in enumerate(kept)})
        slab = (width // 2 + 2,) + tail[1:]
        outs += [shape(slab if m and trip.joined else (len(masks),) + tail, BF16) for m, masks in trip.first]
    places = [trip.rows for trip in trips]
    if len(trips) == 1:
        video = jnp.concatenate([video[:, h : h + 1] for h in trips[0].rows], 1)
        places = [(0, 1)]
    body = functools.partial(part_body, trips, places)
    scratch = [pltpu.VMEM((width + 2, 2 * frames, channels), BF16)]
    me, *parts = on_core(body, outs, me, [video], scratch, limit=24)
    for trip in trips:
        trip.arrays.append(parts.pop(0))
        trip.swap([parts.pop(0) for _ in trip.first[1:]])
    return me


def widen(wide, row, column, cells):
    channels = cells.shape[1]
    frame = lax.broadcasted_iota(jnp.int32, cells.shape, 0)
    for tap in range(TAPS):
        back = TAPS - 1 - tap
        moved = cells
        if back:
            moved = jnp.where(frame < back, 0.0, pltpu.roll(cells, back, 0))
        wide[row, column, :, tap * channels : (tap + 1) * channels] = moved.astype(BF16)


def wavelet_rows(blocks, wide, plain=None):
    count, columns = blocks.shape[:2]
    rows = wide.shape[0]
    frames = blocks.shape[2] // rows

    def column(i, _):
        values = [blocks[b, i].astype(F32) for b in range(count)]
        for level in range(LEVELS):
            span = 1 << level
            later = list(values)
            for b in range(count):
                if not b & span:
                    later[b] = (values[b] + values[b + span]) * inv_root
                    later[b + span] = (values[b] - values[b + span]) * inv_root
            values = later
        for row in range(rows):
            cells = jnp.concatenate([v[row * frames : (row + 1) * frames] for v in values], 0)
            widen(wide, row, i, cells)
            if plain is not None:
                plain[row, i] = cells.astype(BF16)
        return 0

    lax.fori_loop(0, columns, column, 0)


def outer_body(trip, me_ref, *refs):
    *held, wide, plain, blocks = refs
    trip.gather(me_ref[0], held, blocks)
    wavelet_rows(blocks, wide, plain)


def taps(w_ref, terms, before=None):
    columns = terms[0][0].shape[1] - 2
    left, right = [], []
    for wide, row, i in terms:
        for j in range(TAPS):
            cells = wide[row, pl.ds(j, columns)]
            left.append(cells.reshape(-1, cells.shape[-1]))
            right += [w_ref[k, i, j] for k in range(TAPS)]
    total = jnp.dot(
        jnp.concatenate(left, -1), jnp.concatenate(right, 0), preferred_element_type=F32
    )
    if before is not None:
        total = total + before
    return total


def row_sums(total):
    mean = jnp.sum(total, 0, keepdims=True) * (1.0 / total.shape[0])
    apart = total - mean
    return mean, jnp.sum(apart * apart, 0, keepdims=True)


def finish(total, out, sums, row):
    out[row] = total.reshape(out.shape[1:])
    mean, squares = row_sums(total)
    sums[row, 0:1] = mean
    sums[row, 1:2] = squares


def keep(total, out, row):
    out[row] = total.reshape(out.shape[1:])


def flat(ref, row):
    return ref[row].reshape(-1, ref.shape[-1])


def stage_o(me_ref, w_ref, outer, part0, part1):
    keep(taps(w_ref, [(outer, 0, 1)]), part0, 0)
    keep(taps(w_ref, [(outer, 1, 1)]), part0, 1)
    keep(taps(w_ref, [(outer, 0, 0)]), part1, 0)
    keep(taps(w_ref, [(outer, 1, 2)]), part1, 1)


def stage_a(trip, me_ref, w_ref, part1, *refs):
    *held, next1, part2, part3, wide, blocks = refs
    trip.gather(me_ref[0], held, blocks)
    wavelet_rows(blocks, wide)
    keep(taps(w_ref, [(wide, 0, 2)], flat(part1, 0)), next1, 0)
    keep(taps(w_ref, [(wide, 1, 0)], flat(part1, 1)), next1, 1)
    keep(taps(w_ref, [(wide, 0, 1)]), part2, 0)
    keep(taps(w_ref, [(wide, 1, 1)]), part2, 1)
    keep(taps(w_ref, [(wide, 0, 0)]), part3, 0)
    keep(taps(w_ref, [(wide, 1, 2)]), part3, 1)


def stage_b(trip, me_ref, w_ref, above, below, part0, part1, part2, *refs):
    *held, done0, done1, next2, sums, wide, halo, blocks = refs
    trip.gather(me_ref[0], held, blocks)
    wavelet_rows(blocks, wide)

    def column(i, _):
        widen(halo, 0, i, above[i].astype(F32))
        widen(halo, 1, i, below[i].astype(F32))
        return 0

    lax.fori_loop(0, above.shape[0], column, 0)
    finish(taps(w_ref, [(halo, 0, 0), (wide, 0, 2)], flat(part0, 0)), done0, sums, 0)
    finish(taps(w_ref, [(wide, 1, 0), (halo, 1, 2)], flat(part0, 1)), done0, sums, 1)
    finish(taps(w_ref, [(wide, 0, 1)], flat(part1, 0)), done1, sums.at[2:4], 0)
    finish(taps(w_ref, [(wide, 1, 1)], flat(part1, 1)), done1, sums.at[2:4], 1)
    keep(taps(w_ref, [(wide, 0, 0)], flat(part2, 0)), next2, 0)
    keep(taps(w_ref, [(wide, 1, 2)], flat(part2, 1)), next2, 1)


def over_group(values, size):
    lanes = values.shape[-1]
    lane = lax.broadcasted_iota(jnp.int32, values.shape, values.ndim - 1)
    step = 1
    while step < size:
        axis = values.ndim - 1
        down = pltpu.roll(values, step, axis)
        up = pltpu.roll(values, lanes - step, axis)
        values = values + jnp.where((lane & step) != 0, down, up)
        step *= 2
    return values


def stage_c(trip, me_ref, w_ref, part2, part3, earlier, *refs):
    *held, done2, done3, message, sums, wide, blocks = refs
    trip.gather(me_ref[0], held, blocks)
    wavelet_rows(blocks, wide)
    finish(taps(w_ref, [(wide, 0, 2)], flat(part2, 0)), done2, sums, 0)
    finish(taps(w_ref, [(wide, 1, 0)], flat(part2, 1)), done2, sums, 1)
    finish(taps(w_ref, [(wide, 0, 1), (wide, 1, 2)], flat(part3, 0)), done3, sums.at[2:4], 0)
    finish(taps(w_ref, [(wide, 0, 0), (wide, 1, 1)], flat(part3, 1)), done3, sums.at[2:4], 1)
    rows = [sums[r] for r in range(4)]
    rows += [earlier[r] for r in range(4)]
    entries = wide.shape[2] * (wide.shape[1] - 2)
    mean = sum(r[0:1] for r in rows) * (1.0 / len(rows))
    squares = sum(r[1:2] + entries * (r[0:1] - mean) * (r[0:1] - mean) for r in rows)
    lanes = message.shape[-1]
    halves = range(0, mean.shape[1], lanes)
    mean = jnp.concatenate([mean[:, c : c + lanes] for c in halves], 0)
    squares = jnp.concatenate([squares[:, c : c + lanes] for c in halves], 0)
    size = mean.size // GROUPS
    group_mean = over_group(mean, size) * (1.0 / size)
    apart = mean - group_mean
    group = over_group(squares + (entries * len(rows)) * apart * apart, size)
    slot = lax.broadcasted_iota(jnp.int32, (1, lanes), 1) % size
    packed = jnp.zeros((1, lanes), F32)
    for i, value in enumerate([group_mean[0:1], group_mean[1:2], group[0:1], group[1:2]]):
        packed = jnp.where(slot == i, value, packed)
    message[...] = jnp.broadcast_to(packed[None], message.shape)


def norm_body(entries, size, all_ref, gain_ref, bias_ref, *refs):
    *rows, out, affine = refs

    @pl.when(pl.program_id(0) == 0)
    def _():
        devices = all_ref.shape[0]
        given = all_ref[:, 0]
        half = gain_ref.shape[0]
        total = jnp.sum(given, 0, keepdims=True)
        apart = given - total * (1.0 / devices)
        spread = jnp.sum(apart * apart, 0, keepdims=True)
        slot = lax.broadcasted_iota(jnp.int32, total.shape, 1) % size

        def of(values, i):
            return over_group(jnp.where(slot == i, values, 0.0), size)

        group_mean = jnp.concatenate([of(total, p) for p in range(half)], 0) * (1.0 / devices)
        squares = [of(total, half + p) + (entries * size) * of(spread, p) for p in range(half)]
        variance = jnp.concatenate(squares, 0) * (1.0 / (entries * devices * size))
        scale = (0.5 * gain_ref[...]) / jnp.sqrt(variance + 1e-05)
        for p in range(half):
            lanes = slice(p * scale.shape[1], (p + 1) * scale.shape[1])
            affine[0:1, lanes] = group_mean[p : p + 1]
            affine[1:2, lanes] = scale[p : p + 1]
            affine[2:3, lanes] = 0.5 * bias_ref[p : p + 1]

    mean, scale, bias = affine[0:1], affine[1:2], affine[2:3]
    channels = mean.shape[1]
    height = 2 * len(rows)
    for h in range(height):
        ref, place = (rows[h], 0) if h < len(rows) else (rows[height - 1 - h], 1)
        for w in range(2 * out.shape[1]):
            half_v = (ref[place, pl.program_id(0) * (2 * out.shape[1]) + w] - mean) * scale + bias
            value = half_v + half_v * jnp.tanh(half_v)
            lanes = (h % 2 * 2 + w % 2) * channels
            out[h // 2, w // 2, :, lanes : lanes + channels] = value.astype(BF16)


def per_device(video, conv_weight, norm_gain, norm_bias):
    frames, height, width, channels = video.shape
    outputs = conv_weight.shape[-1]
    count = lax.axis_size("tm")
    strips = lax.axis_size("rows")
    devices = count * strips
    columns = width // count
    time = frames * count
    me = lax.axis_index("tm").astype(jnp.int32).reshape(1)
    me = (me, jnp.zeros(MARK.shape, MARK.dtype))
    bits = count.bit_length() - 1
    top, rest = bits - 1, list(range(1, bits - 1))
    outer_trip = Trip((0, 7), [[top], [0] + rest], joined=True)
    third_trip = Trip((2, 5), [[0], [top], rest])
    second_trip = Trip((1, 6), [rest, [0], [top]])
    inner_trip = Trip((3, 4), [[0], rest + [top]])
    trips = [outer_trip, third_trip, second_trip, inner_trip]
    me = part_rows(me, video, trips[:1])
    me = part_rows(me, video, trips[1:])
    me = outer_trip.step(me, flops=3 * 10**9)
    me = third_trip.step(me)
    me = second_trip.step(me, after=[inner_trip.arrays[-1]])
    for trip in (third_trip, second_trip):
        me = trip.step(me)

    def blocks(rows):
        return pltpu.VMEM((count, columns + 2, rows * frames, channels), BF16)

    def wide(rows):
        return (rows, columns + 2, time, TAPS * channels)

    row_pair = shape((2, columns, time, outputs), F32)
    four_sums = shape((4, 2, outputs), F32)

    me, outer, plain = on_core(
        functools.partial(outer_body, outer_trip),
        [shape(wide(2), BF16), shape((2, columns + 2, time, channels), BF16)],
        me,
        outer_trip.arrays,
        [blocks(2)],
    )
    down = [(i, i + 1) for i in range(strips - 1)]
    up = [(i + 1, i) for i in range(strips - 1)]
    above = lax.ppermute(plain[1], "rows", down)
    below = lax.ppermute(plain[0], "rows", up)
    me, part0, part1 = on_core(stage_o, [row_pair, row_pair], me, [conv_weight, outer])
    me = inner_trip.step(me)
    me, part1, part2, part3 = on_core(
        functools.partial(stage_a, third_trip),
        [row_pair, row_pair, row_pair],
        me,
        [conv_weight, part1] + third_trip.arrays,
        [pltpu.VMEM(wide(2), BF16), blocks(2)],
    )
    me, done0, done1, part2, sums = on_core(
        functools.partial(stage_b, second_trip),
        [row_pair, row_pair, row_pair, four_sums],
        me,
        [conv_weight, above, below, part0, part1, part2] + second_trip.arrays,
        [pltpu.VMEM(wide(2), BF16), pltpu.VMEM(wide(2), BF16), blocks(2)],
    )
    me, done2, done3, message = on_core(
        functools.partial(stage_c, inner_trip),
        [row_pair, row_pair, shape((devices, 1, 128), F32)],
        me,
        [conv_weight, part2, part3, sums] + inner_trip.arrays,
        [pltpu.VMEM((4, 2, outputs), F32), pltpu.VMEM(wide(2), BF16), blocks(2)],
    )
    messages = lax.all_to_all(message, ("tm", "rows"), 0, 0, tiled=True)

    steps = columns // 2 // min(2, columns // 2)
    block = columns // steps
    return pl.pallas_call(
        functools.partial(norm_body, float(height * columns * time), outputs // GROUPS),
        grid=(steps,),
        out_shape=shape((height // 2, columns // 2, time, 4 * outputs), BF16),
        in_specs=[VMEM] * 7,
        out_specs=pl.BlockSpec((height // 2, block // 2, time, 4 * outputs), lambda g: (0, g, 0, 0)),
        scratch_shapes=[pltpu.VMEM((8, outputs), F32)],
        compiler_params=pltpu.CompilerParams(vmem_limit_bytes=40 * MIB),
    )(messages, norm_gain.reshape(-1, 128), norm_bias.reshape(-1, 128), done0, done1, done2, done3)


def solution(mesh):
    placed = (P("tm", "rows", None, None), P(), P(), P())
    return jax.shard_map(
        per_device,
        mesh=mesh,
        in_specs=placed,
        out_specs=P("rows", "tm", None, None),
        check_vma=False,
    )
```
